256 devices in a mesh: tower: 8 (over x, y_hi), shard: 32 (over y_lo, z, core).
Axes of the slice: x: 4, y: 4 (y_hi: 2, y_lo: 2; y = y_hi * 2 + y_lo), z: 8, core: 2. Of those that a mesh axis runs over, the one named last changes fastest.
Arguments:
- pooled: bfloat16 [8, 512, 12800], P('tower', 'shard'), may hold values from -6 to 6
- dout: bfloat16 [512, 8, 512], P(('tower', 'shard')), may hold values from -6 to 6
- w_first: bfloat16 [8, 4096, 12800], P('tower', 'shard'), may hold values from -0.0546875 to 0.0546875
- w_second: bfloat16 [8, 4096, 512], P('tower', 'shard'), may hold values from -0.09375 to 0.09375
- table: float32 [8, 32768, 128], P('tower', 'shard'), may hold values from -6 to 6
- accum: float32 [8, 32768], P('tower', 'shard'), may hold values from 0.1 to 10
- touched_ids: int32 [8, 8192], P('tower', 'shard'), may hold values from 0 to 1023, as said below
- lookup_bag: int32 [8, 32, 32, 400], P('tower'), may hold values from 0 to 1599
- lookup_slot: int32 [8, 32, 32, 400], P('tower'), may hold values from 0 to 255
Outputs:
- grad_first: float32 [8, 4096, 12800], P('tower', 'shard')
- grad_second: float32 [8, 4096, 512], P('tower', 'shard')
- new_rows: float32 [8, 8192, 128], P('tower', 'shard')
- new_accum: float32 [8, 8192], P('tower', 'shard')
The draws below stay inside these ranges and needn't reach their ends.
Inputs may be any that keep to these rules, and one draw needn't show every extreme that they name: `touched_ids`: the 256 row numbers of one device are distinct and include 0 and 1023.
All inputs are finite; a program needn't handle non-finite values.
Results may differ from the reference program's by a relative error of at most 0.0029.
Values may be sent and summed in bfloat16 or wider, within the bound.
A program may use at most 128 MiB of HBM per device.

```python
import math
import jax
import jax.numpy as jnp
from jax import lax

EMB = 128
HID = 4096
OUT = 512
FEAT = 100
B_DEV = 2
ROWS_DEV = 1024
TOWERS = 8
IN = 12800
BATCH = 512
TROWS = 32768
TOUCHED = 256
LOOK = 400
N_SHARD = 32


def one_device_rows(key):
    first = jax.random.fold_in(key, 1)
    second = jax.random.fold_in(key, 2)
    middle = jax.random.permutation(first, ROWS_DEV - 2)[:TOUCHED - 2] + 1
    chosen = jnp.concatenate([jnp.zeros((1,), jnp.int32), jnp.full((1,), ROWS_DEV - 1, jnp.int32), middle.astype(jnp.int32)])
    return chosen[jax.random.permutation(second, TOUCHED)]


def draw_touched_ids(key, part):
    key = jax.random.fold_in(key, 7)
    keys = jax.random.split(key, TOWERS * N_SHARD)
    rows = jax.vmap(one_device_rows)(keys)
    return rows.reshape(TOWERS, N_SHARD * TOUCHED).astype(jnp.int32)


def place_ends(array, rng, smallest, largest):
    longest = array.shape.index(max(array.shape))
    spots = []
    for shift in (0, 1):
        where = [jax.random.randint(jax.random.fold_in(rng, axis), (), 0, length) for axis, length in enumerate(array.shape)]
        where[longest] = (where[longest] + shift) % array.shape[longest]
        spots.append(tuple(where))
    return array.at[spots[0]].set(smallest).at[spots[1]].set(largest)


def block_scale(rng, dims, shards, smallest, high):
    loudness, own = 1.0, jax.random.fold_in(rng, 6)
    for axis_at, blocks in shards:
        steps = jnp.exp(jax.random.uniform(jax.random.fold_in(own, axis_at), (blocks,), jnp.float32, smallest / len(shards), high / len(shards)))
        loudness = loudness * jnp.repeat(steps, dims[axis_at] // blocks).reshape([-1 if axis == axis_at else 1 for axis in range(len(dims))])
    return loudness


def scatter_about(own_key, shape, spread, reach, shards=(), kind=jnp.bfloat16):
    loudness = block_scale(own_key, shape, shards, -0.22, 0.18) if shards else 1.0
    array = jax.random.normal(own_key, shape, jnp.float32) * spread * loudness
    return jnp.minimum(jnp.maximum(array, -reach), reach).astype(kind)


def setup_inputs(seed: int = 0) -> dict:
    key_list = jax.random.split(jax.random.key(seed), 10)
    pooled = scatter_about(key_list[0], (TOWERS, BATCH, IN), 1.0, 6.0, ((0, 8), (1, 32)))
    dout = scatter_about(key_list[1], (BATCH, TOWERS, OUT), 1.0, 6.0, ((0, 256),))
    w_first = scatter_about(key_list[2], (TOWERS, HID, IN), IN ** -0.5, 0.0546875, ((0, 8), (1, 32)))
    w_second = scatter_about(key_list[3], (TOWERS, HID, OUT), HID ** -0.5, 0.09375, ((0, 8), (1, 32)))
    table = scatter_about(key_list[4], (TOWERS, TROWS, EMB), 1.0, 6.0, ((0, 8), (1, 32)), jnp.float32)
    accum = jnp.clip(jnp.exp(math.log(10.0) - 4.6051702 * jax.random.uniform(key_list[5], (TOWERS, TROWS), jnp.float32) ** block_scale(key_list[5], (TOWERS, TROWS), ((0, 8), (1, 32)), -0.2, 0.2)), 0.1, 10.0)
    touched_ids = draw_touched_ids(jax.random.fold_in(key_list[9], 71), 0)
    lookup_bag = place_ends(jax.random.randint(key_list[7], (TOWERS, N_SHARD, N_SHARD, LOOK), 0, B_DEV * TOWERS * FEAT), jax.random.fold_in(key_list[7], 1), 0, (B_DEV * TOWERS * FEAT) - 1).astype(jnp.int32)
    lookup_slot = place_ends(jax.random.randint(key_list[8], (TOWERS, N_SHARD, N_SHARD, LOOK), 0, TOUCHED), jax.random.fold_in(key_list[8], 1), 0, TOUCHED - 1).astype(jnp.int32)
    return {"pooled": pooled, "dout": dout, "w_first": w_first, "w_second": w_second, "table": table, "accum": accum, "touched_ids": touched_ids, "lookup_bag": lookup_bag, "lookup_slot": lookup_slot}


def tower_backward(x, grad_out, w_first, w_second, scale):
    pre = lax.dot_general(x, w_first, (((1,), (1,)), ((), ())), preferred_element_type=jnp.float32)
    sig = jax.nn.sigmoid(pre)
    hidden = (pre * sig).astype(jnp.bfloat16)
    back_hidden = lax.dot_general(grad_out, w_second, (((1,), (1,)), ((), ())), preferred_element_type=jnp.float32)
    back_pre = (back_hidden * sig * (1.0 + pre * (1.0 - sig))).astype(jnp.bfloat16)
    grad_first = lax.dot_general(back_pre, x, (((0,), (0,)), ((), ())), preferred_element_type=jnp.float32) * scale
    grad_second = lax.dot_general(hidden, grad_out, (((0,), (0,)), ((), ())), preferred_element_type=jnp.float32) * scale
    back_pooled = jnp.dot(back_pre, w_first, preferred_element_type=jnp.float32).astype(jnp.bfloat16)
    return (grad_first, grad_second, back_pooled)

def owner_rows(flat, bags, slots):
    picked = flat[bags.reshape(-1)].astype(jnp.float32)
    return jax.ops.segment_sum(picked, slots.reshape(-1), num_segments=TOUCHED)

def reference(pooled, dout, w_first, w_second, table, accum, touched_ids, lookup_bag, lookup_slot):
    scale = float(BATCH) ** (-0.5)
    group = B_DEV * TOWERS * FEAT
    offsets = (jnp.arange(N_SHARD, dtype=jnp.int32) * group)[:, None]
    firsts, seconds, rows_out, accums_out = ([], [], [], [])
    for tower_id in range(TOWERS):
        grad_out = dout[:, tower_id, :].reshape(TOWERS, N_SHARD, B_DEV, OUT)
        grad_out = jnp.transpose(grad_out, (1, 0, 2, 3)).reshape(BATCH, OUT)
        grad_first, grad_second, back_pooled = tower_backward(pooled[tower_id], grad_out, w_first[tower_id], w_second[tower_id], scale)
        flat = back_pooled.reshape(BATCH * FEAT, EMB)
        bags = lookup_bag[tower_id] + offsets[None, :, :]
        row_grad = jax.vmap(lambda b, s: owner_rows(flat, b, s))(bags, lookup_slot[tower_id])
        ids = touched_ids[tower_id].reshape(N_SHARD, TOUCHED)
        old_rows = jax.vmap(lambda tb, i: tb[i])(table[tower_id].reshape(N_SHARD, ROWS_DEV, EMB), ids)
        old_acc = jax.vmap(lambda ac, i: ac[i])(accum[tower_id].reshape(N_SHARD, ROWS_DEV), ids)
        new_acc = old_acc + lax.optimization_barrier(jnp.mean(row_grad * row_grad, axis=-1))
        new_row = old_rows - 0.5 * row_grad / (jnp.sqrt(new_acc)[..., None] + 1e-08)
        firsts.append(grad_first)
        seconds.append(grad_second)
        rows_out.append(new_row.reshape(N_SHARD * TOUCHED, EMB))
        accums_out.append(new_acc.reshape(N_SHARD * TOUCHED))
    return (jnp.stack(firsts), jnp.stack(seconds), jnp.stack(rows_out), jnp.stack(accums_out))
```

```python
import jax
import jax.numpy as jnp
from jax import lax
from jax.experimental import pallas as pl
from jax.experimental.pallas import tpu as pltpu
from jax.sharding import PartitionSpec as P

EMB = 128
FEAT = 100
TOUCHED = 256
MESH = pl.DeviceIdType.MESH
VMEM = pltpu.VMEM
DMA = pltpu.SemaphoreType.DMA
NZ = 8
BF = jnp.bfloat16
F32 = jnp.float32


def contract_first(left, right):
    return lax.dot_general(left, right, (((0,), (0,)), ((), ())), preferred_element_type=F32)


def contract_last(left, right):
    return lax.dot_general(left, right, (((1,), (1,)), ((), ())), preferred_element_type=F32)


def place():
    s = lax.axis_index("shard")
    return s, s // 16, (s // 2) % NZ, s % 2


def shard_of(y, z, c):
    return y * 16 + z * 2 + c


def shard_id(s):
    return {"shard": s}


def remote(src, dst, send, recv, where):
    return pltpu.make_async_remote_copy(
        src_ref=src, dst_ref=dst, send_sem=send, recv_sem=recv, device_id=where, device_id_type=MESH
    )


def gather_kernel(
    pooled, w, dout, bags, slots,
    big, gall, wq, counts,
    bag_v, slot_v, dgot, gown, stage,
    in_sem, dsend, drecv, loc_sem, out_sem,
    first_send, first_recv, ring_send, ring_recv, mate_send, mate_recv, wsend, wrecv,
):
    t = lax.axis_index("tower")
    s, y, z, c = place()
    towers = dout.shape[0]
    cols = pooled.shape[1]
    quarter = wq.shape[1]
    half = cols // 2
    mate, other, diag = shard_of(y, z, 1 - c), shard_of(1 - y, z, c), shard_of(1 - y, z, 1 - c)
    ahead, behind = shard_of(y, (z + 1) % NZ, c), shard_of(y, (z + NZ - 1) % NZ, c)

    load_bags = pltpu.make_async_copy(bags, bag_v, in_sem.at[0])
    load_slots = pltpu.make_async_copy(slots, slot_v, in_sem.at[1])
    load_bags.start()
    load_slots.start()

    barrier = pltpu.get_barrier_semaphore()
    for peer in (mate, other, diag, ahead, behind):
        pl.semaphore_signal(barrier, inc=1, device_id=shard_id(peer), device_id_type=MESH)
    for step in range(1, towers):
        pl.semaphore_signal(barrier, inc=1, device_id={"tower": (t + step) % towers}, device_id_type=MESH)
    pl.semaphore_wait(barrier, 5 + towers - 1)

    sent = []

    def block(zz, yy):
        return zz * 4 + yy * 2 + c

    def go(copy):
        copy.start()
        sent.append(copy)
        return copy

    mine = block(z, y)
    tile_rows = dout.shape[1]
    land = dgot.at[pl.ds(pl.multiple_of(t * tile_rows, tile_rows), tile_rows), :]
    dcopies = []
    for step in range(1, towers):
        u = (t + step) % towers
        dcopies.append(go(remote(dout.at[u], land, dsend.at[step], drecv.at[step], {"tower": u})))
    own_d = pltpu.make_async_copy(dout.at[t], land, loc_sem.at[0])
    own_d.start()

    firsts = []
    for i, peer in enumerate((ahead, behind, other)):
        firsts.append(go(remote(pooled, big.at[mine], first_send.at[0, i], first_recv.at[0, i], shard_id(peer))))
    mates = [go(remote(pooled, big.at[mine], mate_send.at[0, 0], mate_recv.at[0, 0], shard_id(mate)))]
    own_p = pltpu.make_async_copy(pooled, big.at[mine], loc_sem.at[1])
    own_p.start()

    own_d.wait()
    for copy in dcopies:
        copy.wait_recv()
    per = gown.shape[1] // EMB
    rows = gown.shape[0]
    for k in range(per):
        gown[:, k * EMB:(k + 1) * EMB] = dgot[pl.ds(k, rows, stride=per), :].astype(BF)
    for i, peer in enumerate((ahead, behind, other)):
        firsts.append(go(remote(gown, gall.at[mine], first_send.at[1, i], first_recv.at[1, i], shard_id(peer))))
    mates.append(go(remote(gown, gall.at[mine], mate_send.at[1, 0], mate_recv.at[1, 0], shard_id(mate))))
    own_g = pltpu.make_async_copy(gown, gall.at[mine], loc_sem.at[2])
    own_g.start()

    def view(kind, at):
        if kind == 0:
            return big.at[at]
        if kind == 1:
            return gall.at[at]
        return big.at[at, :, pl.ds((kind - 2) * half, half)]

    mate_slot = [1, 1]

    def to_mate(kind, at):
        row = 1 if kind == 1 else 0
        slot = mate_slot[row]
        mate_slot[row] += 1
        mates.append(go(remote(view(kind, at), view(kind, at), mate_send.at[row, slot], mate_recv.at[row, slot], shard_id(mate))))

    ring = {}

    def to_ring(kind, at, hop, direction, chain):
        row = 1 if kind == 1 else 0
        peer = behind if direction else ahead
        index = (hop - 1) * 4 + direction * 2 + chain
        ring[(row, hop, direction, chain)] = go(remote(
            view(kind, at), view(kind, at), ring_send.at[row, index], ring_recv.at[row, index], shard_id(peer)))

    yblock = block(z, 1 - y)
    firsts[2].wait_recv()
    for direction in range(2):
        to_ring(0, yblock, 1, direction, 1)
    to_mate(0, yblock)
    firsts[5].wait_recv()
    for direction in range(2):
        to_ring(1, yblock, 1, direction, 1)
    to_mate(1, yblock)

    hid = w.shape[0]
    me4 = y * 2 + c
    wcopies = []
    for i, (yy, cc, peer) in enumerate(((y, 1 - c, mate), (1 - y, c, other), (1 - y, 1 - c, diag))):
        part = pl.multiple_of((yy * 2 + cc) * quarter, EMB)
        wcopies.append(go(remote(
            w.at[:, pl.ds(part, quarter)], wq.at[pl.ds(pl.multiple_of(me4 * hid, hid), hid), :],
            wsend.at[i], wrecv.at[i], shard_id(peer))))
    own_w = pltpu.make_async_copy(
        w.at[:, pl.ds(pl.multiple_of(me4 * quarter, EMB), quarter)],
        wq.at[pl.ds(pl.multiple_of(me4 * hid, hid), hid), :], loc_sem.at[3])
    own_w.start()

    load_bags.wait()
    load_slots.wait()
    look = bags.shape[2]
    pad = stage.shape[2] // 4
    local_feat = quarter // EMB
    samples = pooled.shape[0]
    low = me4 * local_feat

    def owner_counts(owner, slot_at):
        @pl.when(owner >= 2)
        def _():
            pltpu.make_async_copy(stage.at[slot_at], counts.at[owner], out_sem.at[slot_at]).wait()

        for i in range(4):
            source = shard_of(i // 2, z, i % 2)
            bag = bag_v[owner, pl.ds(source, 1), :]
            slot = slot_v[owner, pl.ds(source, 1), :]
            sample = (bag * 5243) >> 19
            feat = bag - sample * FEAT - low
            ok = (feat >= 0) & (feat < local_feat)
            bag_local = jnp.where(ok, feat * samples + sample, -1)
            left = (lax.broadcasted_iota(jnp.int32, (TOUCHED, look), 0) == slot).astype(F32).astype(BF)
            right = (lax.broadcasted_iota(jnp.int32, (pad, look), 0) == bag_local).astype(F32).astype(BF)
            stage[slot_at, :, i * pad:(i + 1) * pad] = contract_last(left, right).astype(BF)
        pltpu.make_async_copy(stage.at[slot_at], counts.at[owner], out_sem.at[slot_at]).start()

    owners = bags.shape[0]
    done = [0]

    def count_some(pairs):
        start = done[0]
        done[0] += pairs

        def body(p, carry):
            owner_counts(p * 2, 0)
            owner_counts(p * 2 + 1, 1)
            return carry

        lax.fori_loop(start, start + pairs, body, 0)

    count_some(4)
    for hop in range(1, 4):
        for chain in range(2):
            count_some(2)
            yy = y if chain == 0 else 1 - y
            for direction in range(2):
                zz = (z + hop) % NZ if direction else (z + NZ - hop) % NZ
                at = block(zz, yy)
                if hop == 1 and chain == 0:
                    firsts[direction].wait_recv()
                else:
                    ring[(0, hop, direction, chain)].wait_recv()
                to_ring(0 if hop < 3 else 2 + direction, at, hop + 1, direction, chain)
                to_mate(0, at)
                if hop == 1 and chain == 0:
                    firsts[3 + direction].wait_recv()
                else:
                    ring[(1, hop, direction, chain)].wait_recv()
                if hop < 3 or direction == 0:
                    to_ring(1, at, hop + 1, direction, chain)
                to_mate(1, at)
    zz = (z + 4) % NZ
    for chain in range(2):
        yy = y if chain == 0 else 1 - y
        at = block(zz, yy)
        for direction in range(2):
            ring[(0, 4, direction, chain)].wait_recv()
            to_mate(2 + direction, at)
        ring[(1, 4, 0, chain)].wait_recv()
        to_mate(1, at)
    for copy in mates:
        copy.wait_recv()
    for copy in wcopies:
        copy.wait_recv()
    for copy in sent:
        copy.wait_send()
    for copy in (own_p, own_g, own_w):
        copy.wait()
    for slot_at in range(2):
        pltpu.make_async_copy(stage.at[slot_at], counts.at[owners - 2 + slot_at], out_sem.at[slot_at]).wait()


def gather_all(pooled, w, dout, bags, slots):
    samples, cols = pooled.shape
    hid = w.shape[0]
    out = dout.shape[1] * EMB * dout.shape[0] // samples
    n_shard = bags.shape[0]
    quarter = cols // 4
    local = quarter // EMB * samples
    pad = -(-local // 128) * 128
    pad = max(pad, 512) if local > 256 else pad
    any_spec = pl.BlockSpec(memory_space=pl.ANY)
    return pl.pallas_call(
        gather_kernel,
        out_shape=(
            jax.ShapeDtypeStruct((n_shard, samples, cols), BF),
            jax.ShapeDtypeStruct((n_shard, samples, out), BF),
            jax.ShapeDtypeStruct((4 * hid, quarter), BF),
            jax.ShapeDtypeStruct((n_shard, TOUCHED, 4 * pad), BF),
        ),
        in_specs=[any_spec] * 5,
        out_specs=(any_spec,) * 4,
        scratch_shapes=[
            VMEM(bags.shape, jnp.int32),
            VMEM(slots.shape, jnp.int32),
            VMEM((dout.shape[0] * dout.shape[1], EMB), F32),
            VMEM((samples, out), BF),
            VMEM((2, TOUCHED, 4 * pad), BF),
            DMA((2,)), DMA((8,)), DMA((8,)), DMA((4,)), DMA((2,)),
            DMA((2, 3)), DMA((2, 3)), DMA((2, 16)), DMA((2, 16)), DMA((2, 18)), DMA((2, 18)), DMA((3,)), DMA((3,)),
        ],
        compiler_params=pltpu.CompilerParams(
            collective_id=0, has_side_effects=True, vmem_limit_bytes=48 * 1024 * 1024
        ),
        name="gather",
    )(pooled, w, dout, bags, slots)


def reduce_kernel(
    bp, wq, flat,
    bpall, first, up_send, down_send, up_recv, down_recv, acc,
    bsend, brecv, fsend, frecv, usend, urecv, vsend, vrecv,
):
    s, y, z, c = place()
    mate, other, diag = shard_of(y, z, 1 - c), shard_of(1 - y, z, c), shard_of(1 - y, z, 1 - c)
    ahead, behind = shard_of(y, (z + 1) % NZ, c), shard_of(y, (z + NZ - 1) % NZ, c)
    hid = bp.shape[1]
    quarter = wq.shape[1]
    rows = acc.shape[1]
    cut = (quarter // EMB + 1) // 2 * EMB
    barrier = pltpu.get_barrier_semaphore()
    peers = (mate, other, diag, ahead, behind)
    for peer in peers:
        pl.semaphore_signal(barrier, inc=1, device_id=shard_id(peer), device_id_type=MESH)
    pl.semaphore_wait(barrier, len(peers))
    me4 = pl.multiple_of((y * 2 + c) * hid, hid)
    sent = []

    def go(copy):
        copy.start()
        sent.append(copy)
        return copy

    got = [
        go(remote(bp, bpall.at[:, pl.ds(me4, hid)], bsend.at[i], brecv.at[i], shard_id(peer)))
        for i, peer in enumerate((other, diag, mate))
    ]
    bpall[:, pl.ds(me4, hid)] = bp[...]
    for copy in got:
        copy.wait_recv()

    tile = quarter // 5 if quarter % (5 * EMB) == 0 else EMB
    tiles = quarter // tile

    def product(slab, write):
        left = bpall[pl.ds(pl.multiple_of(slab * rows, rows), rows), :]

        def body(i, carry):
            at = pl.multiple_of(i * tile, EMB)
            write(at, jnp.dot(left, wq[:, pl.ds(at, tile)], preferred_element_type=F32))
            return carry

        lax.fori_loop(0, tiles, body, 0)

    def into_first(at, value):
        first[:, pl.ds(at, tile)] = value.astype(BF)

    def into_acc(which):
        def write(at, value):
            acc[which, :, pl.ds(at, tile)] = value
        return write

    product((z + 4) % NZ, into_first)
    arriving = [
        go(remote(first.at[:, :cut], up_recv.at[0, :, pl.ds(0, cut)], fsend.at[0], frecv.at[0], shard_id(ahead))),
        go(remote(first.at[:, cut:], down_recv.at[0, :, pl.ds(cut, quarter - cut)], fsend.at[1], frecv.at[1], shard_id(behind))),
    ]
    for k in range(3):
        hop = 3 - k
        product((z + hop) % NZ, into_acc(0))
        product((z + NZ - hop) % NZ, into_acc(1))
        arriving[0].wait_recv()
        if k == 0:
            up_send[k, :, :cut] = (acc[0, :, :cut] + up_recv[k, :, :cut].astype(F32)).astype(BF)
            up_send[k, :, cut:] = acc[0, :, cut:].astype(BF)
        else:
            up_send[k] = (acc[0] + up_recv[k].astype(F32)).astype(BF)
        up = go(remote(up_send.at[k], up_recv.at[k + 1], usend.at[k], urecv.at[k], shard_id(ahead)))
        arriving[1].wait_recv()
        if k == 0:
            down_send[k, :, cut:] = (acc[1, :, cut:] + down_recv[k, :, cut:].astype(F32)).astype(BF)
            down_send[k, :, :cut] = acc[1, :, :cut].astype(BF)
        else:
            down_send[k] = (acc[1] + down_recv[k].astype(F32)).astype(BF)
        down = go(remote(down_send.at[k], down_recv.at[k + 1], vsend.at[k], vrecv.at[k], shard_id(behind)))
        arriving = [up, down]
    product(z, into_acc(0))
    flat[...] = jnp.zeros_like(flat)
    for copy in arriving:
        copy.wait_recv()
    samples = rows // 4
    for f in range(quarter // EMB):
        at = slice(f * EMB, (f + 1) * EMB)
        total = acc[0, :, at] + up_recv[3, :, at].astype(F32) + down_recv[3, :, at].astype(F32)
        total = total.astype(BF)
        for i in range(4):
            flat[i, f * samples:(f + 1) * samples, :] = total[i * samples:(i + 1) * samples]
    for copy in sent:
        copy.wait_send()


def reduce_all(bp, wq, pad, samples):
    batch, hid = bp.shape
    quarter = wq.shape[1]
    rows = 4 * samples
    vm = pl.BlockSpec(memory_space=VMEM)
    return pl.pallas_call(
        reduce_kernel,
        out_shape=jax.ShapeDtypeStruct((4, pad, EMB), BF),
        in_specs=[vm, vm],
        out_specs=vm,
        scratch_shapes=[
            VMEM((batch, 4 * hid), BF),
            VMEM((rows, quarter), BF),
            VMEM((3, rows, quarter), BF),
            VMEM((3, rows, quarter), BF),
            VMEM((4, rows, quarter), BF),
            VMEM((4, rows, quarter), BF),
            VMEM((2, rows, quarter), F32),
            DMA((3,)), DMA((3,)), DMA((2,)), DMA((2,)), DMA((3,)), DMA((3,)), DMA((3,)), DMA((3,)),
        ],
        compiler_params=pltpu.CompilerParams(
            collective_id=1, has_side_effects=True, vmem_limit_bytes=48 * 1024 * 1024
        ),
        name="reduce",
    )(bp, wq)


def shards(pooled, dout, w_first, w_second, table, accum, touched_ids, lookup_bag, lookup_slot):
    towers = dout.shape[1]
    samples = pooled.shape[1]
    dtiles = jnp.transpose(dout, (1, 0, 2)).astype(F32).reshape(towers, -1, EMB)
    big, gall, wq, counts = gather_all(pooled[0], w_first[0], dtiles, lookup_bag[0], lookup_slot[0])
    n_shard = big.shape[0]
    inputs_all = big.reshape(n_shard * samples, -1)
    grad_all = gall.reshape(n_shard * samples, -1)
    scale = float(samples * n_shard) ** (-0.5)
    pre = contract_last(inputs_all, w_first[0])
    sig = jax.nn.sigmoid(pre)
    hidden = (pre * sig).astype(BF)
    back_hidden = contract_last(grad_all, w_second[0])
    back_pre = (back_hidden * sig * (1.0 + pre * (1.0 - sig))).astype(BF)
    flat = reduce_all(back_pre, wq, counts.shape[2] // 4, samples)
    partial = jnp.dot(
        counts.reshape(n_shard * TOUCHED, -1), flat.reshape(-1, EMB), preferred_element_type=F32
    )
    row_grad = lax.psum_scatter(partial, "shard", scatter_dimension=0, tiled=True)
    grad_first = contract_first(back_pre, inputs_all) * scale
    grad_second = contract_first(hidden, grad_all) * scale
    row_ids = touched_ids[0]
    old_rows = table[0][row_ids]
    old_acc = accum[0][row_ids]
    new_acc = old_acc + jnp.mean(row_grad * row_grad, axis=-1)
    new_row = old_rows - 0.5 * row_grad / (jnp.sqrt(new_acc)[:, None] + 1e-08)
    return (grad_first[None], grad_second[None], new_row[None], new_acc[None])


def solution(mesh):
    in_specs = (
        P("tower", "shard", None),
        P(("tower", "shard"), None, None),
        P("tower", "shard", None),
        P("tower", "shard", None),
        P("tower", "shard", None),
        P("tower", "shard"),
        P("tower", "shard"),
        P("tower", None, None, None),
        P("tower", None, None, None),
    )
    out_specs = (
        P("tower", "shard", None),
        P("tower", "shard", None),
        P("tower", "shard", None),
        P("tower", "shard"),
    )
    return jax.shard_map(shards, mesh=mesh, in_specs=in_specs, out_specs=out_specs, check_vma=False)
```

```python
import jax
import jax.numpy as jnp
from jax import lax
from jax.experimental import pallas as pl
from jax.experimental.pallas import tpu as pltpu
from jax.sharding import PartitionSpec as P

EMB = 128
FEAT = 100
TOUCHED = 256
MESH = pl.DeviceIdType.MESH
VMEM = pltpu.VMEM
DMA = pltpu.SemaphoreType.DMA
NZ = 8
BF = jnp.bfloat16
F32 = jnp.float32


def contract_first(left, right):
    return lax.dot_general(left, right, (((0,), (0,)), ((), ())), preferred_element_type=F32)


def contract_last(left, right):
    return lax.dot_general(left, right, (((1,), (1,)), ((), ())), preferred_element_type=F32)


def place():
    s = lax.axis_index("shard")
    return s, s // 16, (s // 2) % NZ, s % 2


def shard_of(y, z, c):
    return y * 16 + z * 2 + c


def shard_id(s):
    return {"shard": s}


def remote(src, dst, send, recv, where):
    return pltpu.make_async_remote_copy(
        src_ref=src, dst_ref=dst, send_sem=send, recv_sem=recv, device_id=where, device_id_type=MESH
    )


def gather_kernel(
    pooled, w, dout, bags, slots,
    big, gall, wq, counts,
    bag_v, slot_v, dgot, gown, stage,
    in_sem, dsend, drecv, loc_sem, out_sem,
    first_send, first_recv, ring_send, ring_recv, mate_send, mate_recv, wsend, wrecv,
):
    t = lax.axis_index("tower")
    s, y, z, c = place()
    towers = dout.shape[0]
    cols = pooled.shape[1]
    quarter = wq.shape[1]
    half = cols // 2
    mate, other, diag = shard_of(y, z, 1 - c), shard_of(1 - y, z, c), shard_of(1 - y, z, 1 - c)
    ahead, behind = shard_of(y, (z + 1) % NZ, c), shard_of(y, (z + NZ - 1) % NZ, c)

    load_bags = pltpu.make_async_copy(bags, bag_v, in_sem.at[0])
    load_slots = pltpu.make_async_copy(slots, slot_v, in_sem.at[1])
    load_bags.start()
    load_slots.start()

    barrier = pltpu.get_barrier_semaphore()
    for peer in (mate, other, diag, ahead, behind):
        pl.semaphore_signal(barrier, inc=1, device_id=shard_id(peer), device_id_type=MESH)
    for step in range(1, towers):
        pl.semaphore_signal(barrier, inc=1, device_id={"tower": (t + step) % towers}, device_id_type=MESH)
    pl.semaphore_wait(barrier, 5 + towers - 1)

    sent = []

    def block(zz, yy):
        return zz * 4 + yy * 2 + c

    def go(copy):
        copy.start()
        sent.append(copy)
        return copy

    mine = block(z, y)
    tile_rows = dout.shape[1]
    land = dgot.at[pl.ds(pl.multiple_of(t * tile_rows, tile_rows), tile_rows), :]
    dcopies = []
    for step in range(1, towers):
        u = (t + step) % towers
        dcopies.append(go(remote(dout.at[u], land, dsend.at[step], drecv.at[step], {"tower": u})))
    own_d = pltpu.make_async_copy(dout.at[t], land, loc_sem.at[0])
    own_d.start()

    firsts = []
    for i, peer in enumerate((ahead, behind, other)):
        firsts.append(go(remote(pooled, big.at[mine], first_send.at[0, i], first_recv.at[0, i], shard_id(peer))))
    mates = [go(remote(pooled, big.at[mine], mate_send.at[0, 0], mate_recv.at[0, 0], shard_id(mate)))]
    own_p = pltpu.make_async_copy(pooled, big.at[mine], loc_sem.at[1])
    own_p.start()

    own_d.wait()
    for copy in dcopies:
        copy.wait_recv()
    per = gown.shape[1] // EMB
    rows = gown.shape[0]
    for k in range(per):
        gown[:, k * EMB:(k + 1) * EMB] = dgot[pl.ds(k, rows, stride=per), :].astype(BF)
    for i, peer in enumerate((ahead, behind, other)):
        firsts.append(go(remote(gown, gall.at[mine], first_send.at[1, i], first_recv.at[1, i], shard_id(peer))))
    mates.append(go(remote(gown, gall.at[mine], mate_send.at[1, 0], mate_recv.at[1, 0], shard_id(mate))))
    own_g = pltpu.make_async_copy(gown, gall.at[mine], loc_sem.at[2])
    own_g.start()

    def view(kind, at):
        if kind == 0:
            return big.at[at]
        if kind == 1:
            return gall.at[at]
        return big.at[at, :, pl.ds((kind - 2) * half, half)]

    mate_slot = [1, 1]

    def to_mate(kind, at):
        row = 1 if kind == 1 else 0
        slot = mate_slot[row]
        mate_slot[row] += 1
        mates.append(go(remote(view(kind, at), view(kind, at), mate_send.at[row, slot], mate_recv.at[row, slot], shard_id(mate))))

    ring = {}

    def to_ring(kind, at, hop, direction, chain):
        row = 1 if kind == 1 else 0
        peer = behind if direction else ahead
        index = (hop - 1) * 4 + direction * 2 + chain
        ring[(row, hop, direction, chain)] = go(remote(
            view(kind, at), view(kind, at), ring_send.at[row, index], ring_recv.at[row, index], shard_id(peer)))

    yblock = block(z, 1 - y)
    firsts[2].wait_recv()
    for direction in range(2):
        to_ring(0, yblock, 1, direction, 1)
    to_mate(0, yblock)
    firsts[5].wait_recv()
    for direction in range(2):
        to_ring(1, yblock, 1, direction, 1)
    to_mate(1, yblock)

    hid = w.shape[0]
    me4 = y * 2 + c
    wcopies = []
    for i, (yy, cc, peer) in enumerate(((y, 1 - c, mate), (1 - y, c, other), (1 - y, 1 - c, diag))):
        part = pl.multiple_of((yy * 2 + cc) * quarter, EMB)
        wcopies.append(go(remote(
            w.at[:, pl.ds(part, quarter)], wq.at[pl.ds(pl.multiple_of(me4 * hid, hid), hid), :],
            wsend.at[i], wrecv.at[i], shard_id(peer))))
    own_w = pltpu.make_async_copy(
        w.at[:, pl.ds(pl.multiple_of(me4 * quarter, EMB), quarter)],
        wq.at[pl.ds(pl.multiple_of(me4 * hid, hid), hid), :], loc_sem.at[3])
    own_w.start()

    load_bags.wait()
    load_slots.wait()
    look = bags.shape[2]
    pad = stage.shape[2] // 4
    local_feat = quarter // EMB
    samples = pooled.shape[0]
    low = me4 * local_feat

    def owner_counts(owner, slot_at):
        @pl.when(owner >= 2)
        def _():
            pltpu.make_async_copy(stage.at[slot_at], counts.at[owner], out_sem.at[slot_at]).wait()

        for i in range(4):
            source = shard_of(i // 2, z, i % 2)
            bag = bag_v[owner, pl.ds(source, 1), :]
            slot = slot_v[owner, pl.ds(source, 1), :]
            sample = (bag * 5243) >> 19
            feat = bag - sample * FEAT - low
            ok = (feat >= 0) & (feat < local_feat)
            bag_local = jnp.where(ok, feat * samples + sample, -1)
            left = (lax.broadcasted_iota(jnp.int32, (TOUCHED, look), 0) == slot).astype(F32).astype(BF)
            right = (lax.broadcasted_iota(jnp.int32, (pad, look), 0) == bag_local).astype(F32).astype(BF)
            stage[slot_at, :, i * pad:(i + 1) * pad] = contract_last(left, right).astype(BF)
        pltpu.make_async_copy(stage.at[slot_at], counts.at[owner], out_sem.at[slot_at]).start()

    owners = bags.shape[0]
    done = [0]

    def count_some(pairs):
        start = done[0]
        done[0] += pairs

        def body(p, carry):
            owner_counts(p * 2, 0)
            owner_counts(p * 2 + 1, 1)
            return carry

        lax.fori_loop(start, start + pairs, body, 0)

    count_some(4)
    for hop in range(1, 4):
        for chain in range(2):
            count_some(2)
            yy = y if chain == 0 else 1 - y
            for direction in range(2):
                zz = (z + hop) % NZ if direction else (z + NZ - hop) % NZ
                at = block(zz, yy)
                if hop == 1 and chain == 0:
                    firsts[direction].wait_recv()
                else:
                    ring[(0, hop, direction, chain)].wait_recv()
                to_ring(0 if hop < 3 else 2 + direction, at, hop + 1, direction, chain)
                to_mate(0, at)
                if hop == 1 and chain == 0:
                    firsts[3 + direction].wait_recv()
                else:
                    ring[(1, hop, direction, chain)].wait_recv()
                if hop < 3 or direction == 0:
                    to_ring(1, at, hop + 1, direction, chain)
                to_mate(1, at)
    zz = (z + 4) % NZ
    for chain in range(2):
        yy = y if chain == 0 else 1 - y
        at = block(zz, yy)
        for direction in range(2):
            ring[(0, 4, direction, chain)].wait_recv()
            to_mate(2 + direction, at)
        ring[(1, 4, 0, chain)].wait_recv()
        to_mate(1, at)
    for copy in mates:
        copy.wait_recv()
    for copy in wcopies:
        copy.wait_recv()
    for copy in sent:
        copy.wait_send()
    for copy in (own_p, own_g, own_w):
        copy.wait()
    for slot_at in range(2):
        pltpu.make_async_copy(stage.at[slot_at], counts.at[owners - 2 + slot_at], out_sem.at[slot_at]).wait()


def gather_all(pooled, w, dout, bags, slots):
    samples, cols = pooled.shape
    hid = w.shape[0]
    out = dout.shape[1] * EMB * dout.shape[0] // samples
    n_shard = bags.shape[0]
    quarter = cols // 4
    local = quarter // EMB * samples
    pad = -(-local // 128) * 128
    pad = max(pad, 512) if local > 256 else pad
    any_spec = pl.BlockSpec(memory_space=pl.ANY)
    return pl.pallas_call(
        gather_kernel,
        out_shape=(
            jax.ShapeDtypeStruct((n_shard, samples, cols), BF),
            jax.ShapeDtypeStruct((n_shard, samples, out), BF),
            jax.ShapeDtypeStruct((4 * hid, quarter), BF),
            jax.ShapeDtypeStruct((n_shard, TOUCHED, 4 * pad), BF),
        ),
        in_specs=[any_spec] * 5,
        out_specs=(any_spec,) * 4,
        scratch_shapes=[
            VMEM(bags.shape, jnp.int32),
            VMEM(slots.shape, jnp.int32),
            VMEM((dout.shape[0] * dout.shape[1], EMB), F32),
            VMEM((samples, out), BF),
            VMEM((2, TOUCHED, 4 * pad), BF),
            DMA((2,)), DMA((8,)), DMA((8,)), DMA((4,)), DMA((2,)),
            DMA((2, 3)), DMA((2, 3)), DMA((2, 16)), DMA((2, 16)), DMA((2, 18)), DMA((2, 18)), DMA((3,)), DMA((3,)),
        ],
        compiler_params=pltpu.CompilerParams(
            collective_id=0, has_side_effects=True, vmem_limit_bytes=58 * 1024 * 1024
        ),
        name="gather",
    )(pooled, w, dout, bags, slots)


def reduce_kernel(
    bp, wq, counts,
    out,
    bpall, acc, send1, recv1, flat, cv, mate_out, mate_in, own_rows, send2, recv2, yout, yin,
    bsend, brecv, ssem1, rsem1, csem, msend, mrecv, ssem2, rsem2, ysem,
):
    s, y, z, c = place()
    mate, other, diag = shard_of(y, z, 1 - c), shard_of(1 - y, z, c), shard_of(1 - y, z, 1 - c)
    peers = (shard_of(y, (z + 1) % NZ, c), shard_of(y, (z + NZ - 1) % NZ, c))
    hid = bp.shape[1]
    quarter = wq.shape[1]
    rows = acc.shape[1]
    samples = rows // 4
    slabs = [(z + step) % NZ for step in (4, 3, 5, 2, 6, 1, 7, 0)]

    def load_counts(n):
        return pltpu.make_async_copy(counts.at[:, slabs[n]], cv.at[n % 4], csem.at[n % 4])

    for n in range(4):
        load_counts(n).start()
    barrier = pltpu.get_barrier_semaphore()
    for peer in (mate, other, diag) + peers:
        pl.semaphore_signal(barrier, inc=1, device_id=shard_id(peer), device_id_type=MESH)
    pl.semaphore_wait(barrier, 5)
    me4 = pl.multiple_of((y * 2 + c) * hid, hid)
    sent = []

    def go(copy):
        copy.start()
        sent.append(copy)
        return copy

    got_bp = [
        go(remote(bp, bpall.at[:, pl.ds(me4, hid)], bsend.at[i], brecv.at[i], shard_id(peer)))
        for i, peer in enumerate((other, diag, mate))
    ]
    bpall[:, pl.ds(me4, hid)] = bp[...]
    flat[...] = jnp.zeros_like(flat)
    for copy in got_bp:
        copy.wait_recv()

    def ring(view, calc, own, send, recv, ssem, rsem):
        copies = {}

        def push(direction, h, part, value):
            place_at = view(send, direction, h, part)
            place_at[...] = value.astype(send.dtype)
            index = h * 2 + part
            copies[(direction, h, part)] = go(remote(
                place_at, view(recv, direction, h, part),
                ssem.at[direction, index], rsem.at[direction, index], shard_id(peers[direction])))

        def got(direction, h, part):
            copies[(direction, h, part)].wait_recv()
            return view(recv, direction, h, part)[...].astype(F32)

        calc(0)
        push(0, 0, 0, own(0, 0))
        push(1, 0, 1, own(0, 1))
        calc(1)
        calc(2)
        push(0, 1, 1, own(1, 1))
        push(1, 1, 0, own(2, 0))
        calc(3)
        calc(4)
        push(0, 1, 0, own(1, 0) + got(0, 0, 0))
        push(1, 1, 1, own(2, 1) + got(1, 0, 1))
        calc(5)
        calc(6)
        for h in (2, 3):
            n = 2 * h - 1
            push(0, h, 1, own(n, 1) + got(0, h - 1, 1))
            push(1, h, 0, own(n + 1, 0) + got(1, h - 1, 0))
            push(0, h, 0, own(n, 0) + got(0, h - 1, 0))
            push(1, h, 1, own(n + 1, 1) + got(1, h - 1, 1))
            if h == 2:
                calc(7)

        def final(part):
            return own(7, part) + got(0, 3, part) + got(1, 3, part)

        return final

    tile = quarter // 5 if quarter % (5 * EMB) == 0 else EMB
    cut = (quarter // EMB + 1) // 2 * EMB
    spans = ((0, cut), (cut, quarter))

    def product(n):
        left = bpall[pl.ds(pl.multiple_of(slabs[n] * rows, rows), rows), :]

        def body(i, carry):
            at = pl.ds(pl.multiple_of(i * tile, EMB), tile)
            acc[n % 4, :, at] = jnp.dot(left, wq[:, at], preferred_element_type=F32)
            return carry

        lax.fori_loop(0, quarter // tile, body, 0)

    def view1(buf, direction, h, part):
        return buf.at[direction, h, :, spans[part][0]:spans[part][1]]

    def own1(n, part):
        return acc[n % 4, :, spans[part][0]:spans[part][1]]

    final = ring(view1, product, own1, send1, recv1, ssem1, rsem1)
    for part in (1, 0):
        total = final(part).astype(BF)
        for f in range(spans[part][0] // EMB, spans[part][1] // EMB):
            at = f * EMB - spans[part][0]
            for i in range(4):
                flat[i, f * samples:(f + 1) * samples, :] = total[i * samples:(i + 1) * samples, at:at + EMB]

    bags = flat.shape[0] * flat.shape[1]
    mates = {}

    def row_sums(n):
        load_counts(n).wait()
        for yy in range(2):
            mate_out[n, yy] = jnp.dot(cv[n % 4, yy, 1 - c], flat[...].reshape(bags, EMB), preferred_element_type=F32)
        mates[n] = go(remote(mate_out.at[n], mate_in.at[n], msend.at[n], mrecv.at[n], shard_id(mate)))
        for yy in range(2):
            own_rows[n, yy] = jnp.dot(cv[n % 4, yy, c], flat[...].reshape(bags, EMB), preferred_element_type=F32)
        if n + 4 < 8:
            load_counts(n + 4).start()

    def calc2(n):
        if n == 0:
            row_sums(0)
            row_sums(1)
        elif n > 1:
            row_sums(n)

    def view2(buf, direction, h, part):
        return buf.at[direction, h, part]

    def own2(n, part):
        if n in mates:
            mates.pop(n).wait_recv()
        return own_rows[n, part] + mate_in[n, part]

    final = ring(view2, calc2, own2, send2, recv2, ssem2, rsem2)
    sums = [final(0), final(1)]
    yout[...] = jnp.where(y == 0, sums[1], sums[0])
    last = go(remote(yout, yin, ysem.at[0], ysem.at[1], shard_id(other)))
    mine = jnp.where(y == 0, sums[0], sums[1])
    last.wait_recv()
    out[...] = mine + yin[...]
    for copy in sent:
        copy.wait_send()


def reduce_all(bp, wq, counts, samples):
    batch, hid = bp.shape
    quarter = wq.shape[1]
    rows = 4 * samples
    owners, touched, width = counts.shape
    vm = pl.BlockSpec(memory_space=VMEM)
    return pl.pallas_call(
        reduce_kernel,
        out_shape=jax.ShapeDtypeStruct((touched, EMB), F32),
        in_specs=[vm, vm, pl.BlockSpec(memory_space=pl.ANY)],
        out_specs=vm,
        scratch_shapes=[
            VMEM((batch, 4 * hid), BF),
            VMEM((4, rows, quarter), F32),
            VMEM((2, 4, rows, quarter), BF),
            VMEM((2, 4, rows, quarter), BF),
            VMEM((4, width // 4, EMB), BF),
            VMEM((4, 2, 2, touched, width), BF),
            VMEM((8, 2, touched, EMB), F32),
            VMEM((8, 2, touched, EMB), F32),
            VMEM((8, 2, touched, EMB), F32),
            VMEM((2, 4, 2, touched, EMB), F32),
            VMEM((2, 4, 2, touched, EMB), F32),
            VMEM((touched, EMB), F32),
            VMEM((touched, EMB), F32),
            DMA((3,)), DMA((3,)), DMA((2, 8)), DMA((2, 8)), DMA((4,)), DMA((8,)), DMA((8,)), DMA((2, 8)), DMA((2, 8)),
            DMA((2,)),
        ],
        compiler_params=pltpu.CompilerParams(
            collective_id=1, has_side_effects=True, vmem_limit_bytes=58 * 1024 * 1024
        ),
        name="reduce",
    )(bp, wq, counts.reshape(2, NZ, 2, touched, width))


def shards(pooled, dout, w_first, w_second, table, accum, touched_ids, lookup_bag, lookup_slot):
    towers = dout.shape[1]
    samples = pooled.shape[1]
    dtiles = jnp.transpose(dout, (1, 0, 2)).astype(F32).reshape(towers, -1, EMB)
    big, gall, wq, counts = gather_all(pooled[0], w_first[0], dtiles, lookup_bag[0], lookup_slot[0])
    n_shard = big.shape[0]
    inputs_all = big.reshape(n_shard * samples, -1)
    grad_all = gall.reshape(n_shard * samples, -1)
    scale = float(samples * n_shard) ** (-0.5)
    pre = contract_last(inputs_all, w_first[0])
    sig = jax.nn.sigmoid(pre)
    hidden = (pre * sig).astype(BF)
    back_hidden = contract_last(grad_all, w_second[0])
    back_pre = (back_hidden * sig * (1.0 + pre * (1.0 - sig))).astype(BF)
    row_grad = reduce_all(back_pre, wq, counts, samples)
    grad_first = contract_first(back_pre, inputs_all) * scale
    grad_second = contract_first(hidden, grad_all) * scale
    row_ids = touched_ids[0]
    old_rows = table[0][row_ids]
    old_acc = accum[0][row_ids]
    new_acc = old_acc + jnp.mean(row_grad * row_grad, axis=-1)
    new_row = old_rows - 0.5 * row_grad / (jnp.sqrt(new_acc)[:, None] + 1e-08)
    return (grad_first[None], grad_second[None], new_row[None], new_acc[None])


def solution(mesh):
    in_specs = (
        P("tower", "shard", None),
        P(("tower", "shard"), None, None),
        P("tower", "shard", None),
        P("tower", "shard", None),
        P("tower", "shard", None),
        P("tower", "shard"),
        P("tower", "shard"),
        P("tower", None, None, None),
        P("tower", None, None, None),
    )
    out_specs = (
        P("tower", "shard", None),
        P("tower", "shard", None),
        P("tower", "shard", None),
        P("tower", "shard"),
    )
    return jax.shard_map(shards, mesh=mesh, in_specs=in_specs, out_specs=out_specs, check_vma=False)
```

```python
import jax
import jax.numpy as jnp
from jax import lax
from jax.experimental import pallas as pl
from jax.experimental.pallas import tpu as pltpu
from jax.sharding import PartitionSpec as P

EMB = 128
FEAT = 100
TOUCHED = 256
MESH = pl.DeviceIdType.MESH
VMEM = pltpu.VMEM
DMA = pltpu.SemaphoreType.DMA
NZ = 8
BF = jnp.bfloat16
F32 = jnp.float32


def contract_first(left, right):
    return lax.dot_general(left, right, (((0,), (0,)), ((), ())), preferred_element_type=F32)


def contract_last(left, right):
    return lax.dot_general(left, right, (((1,), (1,)), ((), ())), preferred_element_type=F32)


def place():
    s = lax.axis_index("shard")
    return s, s // 16, (s // 2) % NZ, s % 2


def shard_of(y, z, c):
    return y * 16 + z * 2 + c


def shard_id(s):
    return {"shard": s}


def remote(src, dst, send, recv, where):
    return pltpu.make_async_remote_copy(
        src_ref=src, dst_ref=dst, send_sem=send, recv_sem=recv, device_id=where, device_id_type=MESH
    )


def tower_kernel(
    pooled, w, w2, dout, bags, slots,
    big, counts, gall, bp_out, hid_out, out,
    bag_v, slot_v, dgot, stage, w_v, xblk, wq,
    bpall, acc, send1, recv1, flat, cv, mate_out, mate_in, own_rows, send2, recv2, yout, yin,
    in_sem, dsend, drecv, loc_sem, out_sem, xsem,
    first_send, first_recv, ring_send, ring_recv, mate_send, mate_recv, wsend, wrecv,
    bsend, brecv, ssem1, rsem1, csem, msend, mrecv, ssem2, rsem2, ysem,
):
    t = lax.axis_index("tower")
    s, y, z, c = place()
    towers = dout.shape[0]
    samples, cols = pooled.shape
    hid = w.shape[0]
    quarter = wq.shape[1]
    half = cols // 2
    rows = 4 * samples
    mate, other, diag = shard_of(y, z, 1 - c), shard_of(1 - y, z, c), shard_of(1 - y, z, 1 - c)
    ahead, behind = shard_of(y, (z + 1) % NZ, c), shard_of(y, (z + NZ - 1) % NZ, c)
    peers = (ahead, behind)
    me4 = y * 2 + c
    me_hid = pl.multiple_of(me4 * hid, hid)

    load_w = pltpu.make_async_copy(w, w_v, in_sem.at[2])
    load_bags = pltpu.make_async_copy(bags, bag_v, in_sem.at[0])
    load_slots = pltpu.make_async_copy(slots, slot_v, in_sem.at[1])
    load_bags.start()
    load_slots.start()
    load_w.start()

    barrier = pltpu.get_barrier_semaphore()
    for peer in (mate, other, diag, ahead, behind):
        pl.semaphore_signal(barrier, inc=1, device_id=shard_id(peer), device_id_type=MESH)
    for step in range(1, towers):
        pl.semaphore_signal(barrier, inc=1, device_id={"tower": (t + step) % towers}, device_id_type=MESH)
    pl.semaphore_wait(barrier, 5 + towers - 1)

    sent = []

    def block(zz, yy):
        return zz * 4 + yy * 2 + c

    def go(copy):
        copy.start()
        sent.append(copy)
        return copy

    mine = block(z, y)
    pending = {}

    def note(label, copy):
        pending.setdefault(label, []).append(copy)

    tile_rows = dout.shape[1]
    land = dgot.at[pl.ds(pl.multiple_of(t * tile_rows, tile_rows), tile_rows), :]
    dcopies = []
    for step in range(1, towers):
        u = (t + step) % towers
        dcopies.append(go(remote(dout.at[u], land, dsend.at[step], drecv.at[step], {"tower": u})))
    own_d = pltpu.make_async_copy(dout.at[t], land, loc_sem.at[0])
    own_d.start()

    firsts = []
    for i, peer in enumerate((ahead, behind, other)):
        firsts.append(go(remote(pooled, big.at[mine], first_send.at[0, i], first_recv.at[0, i], shard_id(peer))))
    note(0, go(remote(pooled, big.at[mine], mate_send.at[0, 0], mate_recv.at[0, 0], shard_id(mate))))
    own_p = pltpu.make_async_copy(pooled, big.at[mine], loc_sem.at[1])
    own_p.start()

    own_d.wait()
    for copy in dcopies:
        copy.wait_recv()
    per = gall.shape[2] // EMB
    for k in range(per):
        gall[mine, :, k * EMB:(k + 1) * EMB] = dgot[pl.ds(k, samples, stride=per), :].astype(BF)
    gmine = gall.at[mine]
    for i, peer in enumerate((ahead, behind, other)):
        firsts.append(go(remote(gmine, gmine, first_send.at[1, i], first_recv.at[1, i], shard_id(peer))))
    note(0, go(remote(gmine, gmine, mate_send.at[1, 0], mate_recv.at[1, 0], shard_id(mate))))

    def view(kind, at):
        if kind == 0:
            return big.at[at]
        if kind == 1:
            return gall.at[at]
        return big.at[at, :, pl.ds((kind - 2) * half, half)]

    mate_slot = [1, 1]

    def to_mate(kind, at, label):
        row = 1 if kind == 1 else 0
        slot = mate_slot[row]
        mate_slot[row] += 1
        note(label, go(remote(
            view(kind, at), view(kind, at), mate_send.at[row, slot], mate_recv.at[row, slot], shard_id(mate))))

    ring_copies = {}

    def to_ring(kind, at, hop, direction, chain):
        row = 1 if kind == 1 else 0
        index = (hop - 1) * 4 + direction * 2 + chain
        ring_copies[(row, hop, direction, chain)] = go(remote(
            view(kind, at), view(kind, at), ring_send.at[row, index], ring_recv.at[row, index],
            shard_id(peers[direction])))

    yblock = block(z, 1 - y)
    firsts[2].wait_recv()
    for direction in range(2):
        to_ring(0, yblock, 1, direction, 1)
    to_mate(0, yblock, 0)
    firsts[5].wait_recv()
    for direction in range(2):
        to_ring(1, yblock, 1, direction, 1)
    to_mate(1, yblock, 0)

    wcopies = []
    for i, (yy, cc, peer) in enumerate(((y, 1 - c, mate), (1 - y, c, other), (1 - y, 1 - c, diag))):
        part = pl.multiple_of((yy * 2 + cc) * quarter, EMB)
        wcopies.append(go(remote(
            w.at[:, pl.ds(part, quarter)], wq.at[pl.ds(me_hid, hid), :], wsend.at[i], wrecv.at[i], shard_id(peer))))
    own_w = pltpu.make_async_copy(
        w.at[:, pl.ds(pl.multiple_of(me4 * quarter, EMB), quarter)], wq.at[pl.ds(me_hid, hid), :], loc_sem.at[3])
    own_w.start()

    load_bags.wait()
    load_slots.wait()
    load_w.wait()
    look = bags.shape[2]
    pad = stage.shape[2] // 4
    local_feat = quarter // EMB
    low = me4 * local_feat

    def owner_counts(owner, slot_at):
        @pl.when(owner >= 2)
        def _():
            pltpu.make_async_copy(stage.at[slot_at], counts.at[owner], out_sem.at[slot_at]).wait()

        for i in range(4):
            source = shard_of(i // 2, z, i % 2)
            bag = bag_v[owner, pl.ds(source, 1), :]
            slot = slot_v[owner, pl.ds(source, 1), :]
            sample = (bag * 5243) >> 19
            feat = bag - sample * FEAT - low
            ok = (feat >= 0) & (feat < local_feat)
            bag_local = jnp.where(ok, feat * samples + sample, -1)
            left = (lax.broadcasted_iota(jnp.int32, (TOUCHED, look), 0) == slot).astype(F32).astype(BF)
            right = (lax.broadcasted_iota(jnp.int32, (pad, look), 0) == bag_local).astype(F32).astype(BF)
            stage[slot_at, :, i * pad:(i + 1) * pad] = contract_last(left, right).astype(BF)
        pltpu.make_async_copy(stage.at[slot_at], counts.at[owner], out_sem.at[slot_at]).start()

    owners = bags.shape[0]
    done = [0]

    def count_some(pairs):
        start = done[0]
        done[0] += pairs

        def body(p, carry):
            owner_counts(p * 2, 0)
            owner_counts(p * 2 + 1, 1)
            return carry

        lax.fori_loop(start, start + pairs, body, 0)

    def load_slab(label, zz, at):
        for copy in pending.pop(label):
            copy.wait_recv()
        load = pltpu.make_async_copy(big.at[pl.ds(zz * 4, 4)], xblk.at[at], xsem.at[at])
        load.start()
        return load

    bp_copies = {}
    step_k = cols // 10 if cols % (10 * EMB) == 0 else EMB

    def tower_step(loads, zs, names):
        m = len(zs)
        for load in loads:
            load.wait()

        def body(i, total):
            at = pl.ds(pl.multiple_of(i * step_k, EMB), step_k)
            left = xblk[0:m, :, :, at].reshape(m * rows, step_k)
            return total + contract_last(left, w_v[:, at])

        pre = lax.fori_loop(0, cols // step_k, body, jnp.zeros((m * rows, hid), F32))
        sig = jax.nn.sigmoid(pre)
        hidden = (pre * sig).astype(BF)
        for i, zz in enumerate(zs):
            part = slice(i * rows, (i + 1) * rows)
            at = pl.ds(pl.multiple_of(zz * rows, rows), rows)
            grads = gall[pl.ds(zz * 4, 4)].reshape(rows, gall.shape[2])
            back_hidden = contract_last(grads, w2[...])
            sg, p = sig[part], pre[part]
            back_pre = (back_hidden * sg * (1.0 + p * (1.0 - sg))).astype(BF)
            hid_out[at, :] = hidden[part]
            bp_out[at, :] = back_pre
            bpall[at, pl.ds(me_hid, hid)] = back_pre
            where = bpall.at[at, pl.ds(me_hid, hid)]
            bp_copies[names[i]] = [
                go(remote(where, where, bsend.at[names[i], j], brecv.at[names[i], j], shard_id(peer)))
                for j, peer in enumerate((other, diag, mate))
            ]

    steps = (4, 3, 5, 2, 6, 1, 7, 0)
    slabs = [(z + step) % NZ for step in steps]
    tile = quarter // 5 if quarter % (5 * EMB) == 0 else EMB
    cut = (quarter // EMB + 1) // 2 * EMB
    spans = ((0, cut), (cut, quarter))
    slab_w = list(wcopies)

    def product(n):
        while slab_w:
            slab_w.pop().wait_recv()
        for copy in bp_copies.pop(steps[n]):
            copy.wait_recv()
        left = bpall[pl.ds(pl.multiple_of(slabs[n] * rows, rows), rows), :]

        def body(i, carry):
            at = pl.ds(pl.multiple_of(i * tile, EMB), tile)
            acc[n % 4, :, at] = jnp.dot(left, wq[:, at], preferred_element_type=F32)
            return carry

        lax.fori_loop(0, quarter // tile, body, 0)

    count_some(3)
    own_p.wait()
    loads = [load_slab(0, z, 0)]
    zs, names = [z], [0]
    for hop in range(1, 4):
        for chain in range(2):
            if chain == 1:
                tower_step(loads, zs, names)
            count_some(2)
            yy = y if chain == 0 else 1 - y
            for direction in range(2):
                zz = (z + hop) % NZ if direction else (z + NZ - hop) % NZ
                at = block(zz, yy)
                label = (hop, direction)
                if hop == 1 and chain == 0:
                    firsts[direction].wait_recv()
                else:
                    ring_copies[(0, hop, direction, chain)].wait_recv()
                to_ring(0 if hop < 3 else 2 + direction, at, hop + 1, direction, chain)
                to_mate(0, at, label)
                if hop == 1 and chain == 0:
                    firsts[3 + direction].wait_recv()
                else:
                    ring_copies[(1, hop, direction, chain)].wait_recv()
                if hop < 3 or direction == 0:
                    to_ring(1, at, hop + 1, direction, chain)
                to_mate(1, at, label)
        if hop == 3:
            count_some(1)
        zs = [(z + NZ - hop) % NZ, (z + hop) % NZ]
        names = [NZ - hop, hop]
        loads = [load_slab((hop, direction), zs[direction], direction) for direction in range(2)]
    own_w.wait()
    tower_step(loads, zs, names)
    for slot_at in range(2):
        pltpu.make_async_copy(stage.at[slot_at], counts.at[owners - 2 + slot_at], out_sem.at[slot_at]).wait()

    depth = cv.shape[0]
    grid = counts.reshape(2, NZ, 2, TOUCHED, 4 * pad)

    def load_counts(n):
        return pltpu.make_async_copy(grid.at[:, slabs[n]], cv.at[n % depth], csem.at[n % depth])

    for n in range(depth):
        load_counts(n).start()
    flat[...] = jnp.zeros_like(flat)
    product(1)
    product(2)
    zz = (z + 4) % NZ
    for chain in range(2):
        yy = y if chain == 0 else 1 - y
        at = block(zz, yy)
        for direction in range(2):
            ring_copies[(0, 4, direction, chain)].wait_recv()
            to_mate(2 + direction, at, 4)
        ring_copies[(1, 4, 0, chain)].wait_recv()
        to_mate(1, at, 4)

    def ring(view, calc, own, send, recv, ssem, rsem, early):
        copies = {}

        def push(direction, h, part, value):
            place_at = view(send, direction, h, part)
            place_at[...] = value.astype(send.dtype)
            index = h * 2 + part
            copies[(direction, h, part)] = go(remote(
                place_at, view(recv, direction, h, part),
                ssem.at[direction, index], rsem.at[direction, index], shard_id(peers[direction])))

        def got(direction, h, part):
            copies[(direction, h, part)].wait_recv()
            return view(recv, direction, h, part)[...].astype(F32)

        if early:
            push(0, 1, 1, own(1, 1))
            push(1, 1, 0, own(2, 0))
        calc(0)
        push(0, 0, 0, own(0, 0))
        push(1, 0, 1, own(0, 1))
        if not early:
            calc(1)
            calc(2)
            push(0, 1, 1, own(1, 1))
            push(1, 1, 0, own(2, 0))
        calc(3)
        calc(4)
        push(0, 1, 0, own(1, 0) + got(0, 0, 0))
        push(1, 1, 1, own(2, 1) + got(1, 0, 1))
        calc(5)
        calc(6)
        for h in (2, 3):
            n = 2 * h - 1
            push(0, h, 1, own(n, 1) + got(0, h - 1, 1))
            push(1, h, 0, own(n + 1, 0) + got(1, h - 1, 0))
            push(0, h, 0, own(n, 0) + got(0, h - 1, 0))
            push(1, h, 1, own(n + 1, 1) + got(1, h - 1, 1))
            if h == 2:
                calc(7)

        def final(part):
            return own(7, part) + got(0, 3, part) + got(1, 3, part)

        return final

    def view1(buf, direction, h, part):
        return buf.at[direction, h, :, spans[part][0]:spans[part][1]]

    def own1(n, part):
        return acc[n % 4, :, spans[part][0]:spans[part][1]]

    def calc1(n):
        if n == 0:
            tower_step([load_slab(4, zz, 0)], [zz], [4])
        product(n)

    final = ring(view1, calc1, own1, send1, recv1, ssem1, rsem1, True)
    for part in (1, 0):
        total = final(part).astype(BF)
        for f in range(spans[part][0] // EMB, spans[part][1] // EMB):
            at = f * EMB - spans[part][0]
            for i in range(4):
                flat[i, f * samples:(f + 1) * samples, :] = total[i * samples:(i + 1) * samples, at:at + EMB]

    local_bags = flat.shape[0] * flat.shape[1]
    mates = {}

    def row_sums(n):
        load_counts(n).wait()
        for yy in range(2):
            mate_out[n, yy] = jnp.dot(
                cv[n % depth, yy, 1 - c], flat[...].reshape(local_bags, EMB), preferred_element_type=F32)
        mates[n] = go(remote(mate_out.at[n], mate_in.at[n], msend.at[n], mrecv.at[n], shard_id(mate)))
        for yy in range(2):
            own_rows[n, yy] = jnp.dot(
                cv[n % depth, yy, c], flat[...].reshape(local_bags, EMB), preferred_element_type=F32)
        if n + depth < NZ:
            load_counts(n + depth).start()

    def calc2(n):
        if n == 0:
            row_sums(0)
            row_sums(1)
        elif n > 1:
            row_sums(n)

    def view2(buf, direction, h, part):
        return buf.at[direction, h, part]

    def own2(n, part):
        if n in mates:
            mates.pop(n).wait_recv()
        return own_rows[n, part] + mate_in[n, part]

    final = ring(view2, calc2, own2, send2, recv2, ssem2, rsem2, False)
    sums = [final(0), final(1)]
    yout[...] = jnp.where(y == 0, sums[1], sums[0])
    last = go(remote(yout, yin, ysem.at[0], ysem.at[1], shard_id(other)))
    kept = jnp.where(y == 0, sums[0], sums[1])
    last.wait_recv()
    out[...] = kept + yin[...]
    for copy in sent:
        copy.wait_send()


def tower_all(pooled, w, w2, dout, bags, slots):
    samples, cols = pooled.shape
    hid = w.shape[0]
    n_shard = bags.shape[0]
    batch = n_shard * samples
    out = w2.shape[1]
    quarter = cols // 4
    rows = 4 * samples
    pad = -(-(quarter // EMB * samples) // 512) * 512
    any_spec = pl.BlockSpec(memory_space=pl.ANY)
    vm = pl.BlockSpec(memory_space=VMEM)
    depth = 3
    return pl.pallas_call(
        tower_kernel,
        out_shape=(
            jax.ShapeDtypeStruct((n_shard, samples, cols), BF),
            jax.ShapeDtypeStruct((n_shard, TOUCHED, 4 * pad), BF),
            jax.ShapeDtypeStruct((n_shard, samples, out), BF),
            jax.ShapeDtypeStruct((batch, hid), BF),
            jax.ShapeDtypeStruct((batch, hid), BF),
            jax.ShapeDtypeStruct((TOUCHED, EMB), F32),
        ),
        in_specs=[any_spec, any_spec, vm, any_spec, any_spec, any_spec],
        out_specs=(any_spec, any_spec, vm, vm, vm, vm),
        scratch_shapes=[
            VMEM(bags.shape, jnp.int32),
            VMEM(slots.shape, jnp.int32),
            VMEM((dout.shape[0] * dout.shape[1], EMB), F32),
            VMEM((2, TOUCHED, 4 * pad), BF),
            VMEM((hid, cols), BF),
            VMEM((2, 4, samples, cols), BF),
            VMEM((4 * hid, quarter), BF),
            VMEM((batch, 4 * hid), BF),
            VMEM((4, rows, quarter), F32),
            VMEM((2, 4, rows, quarter), BF),
            VMEM((2, 4, rows, quarter), BF),
            VMEM((4, pad, EMB), BF),
            VMEM((depth, 2, 2, TOUCHED, 4 * pad), BF),
            VMEM((NZ, 2, TOUCHED, EMB), F32),
            VMEM((NZ, 2, TOUCHED, EMB), F32),
            VMEM((NZ, 2, TOUCHED, EMB), F32),
            VMEM((2, 4, 2, TOUCHED, EMB), F32),
            VMEM((2, 4, 2, TOUCHED, EMB), F32),
            VMEM((TOUCHED, EMB), F32),
            VMEM((TOUCHED, EMB), F32),
            DMA((3,)), DMA((8,)), DMA((8,)), DMA((4,)), DMA((2,)), DMA((2,)),
            DMA((2, 3)), DMA((2, 3)), DMA((2, 16)), DMA((2, 16)), DMA((2, 18)), DMA((2, 18)), DMA((3,)), DMA((3,)),
            DMA((8, 3)), DMA((8, 3)), DMA((2, 8)), DMA((2, 8)), DMA((depth,)), DMA((8,)), DMA((8,)),
            DMA((2, 8)), DMA((2, 8)), DMA((2,)),
        ],
        compiler_params=pltpu.CompilerParams(
            collective_id=0, has_side_effects=True, vmem_limit_bytes=60 * 1024 * 1024
        ),
        name="tower",
    )(pooled, w, w2, dout, bags, slots)


def shards(pooled, dout, w_first, w_second, table, accum, touched_ids, lookup_bag, lookup_slot):
    towers = dout.shape[1]
    samples = pooled.shape[1]
    dtiles = jnp.transpose(dout, (1, 0, 2)).astype(F32).reshape(towers, -1, EMB)
    big, _, gall, back_pre, hidden, row_grad = tower_all(
        pooled[0], w_first[0], w_second[0], dtiles, lookup_bag[0], lookup_slot[0])
    n_shard = big.shape[0]
    inputs_all = big.reshape(n_shard * samples, -1)
    grad_all = gall.reshape(n_shard * samples, -1)
    scale = float(samples * n_shard) ** (-0.5)
    grad_first = contract_first(back_pre, inputs_all) * scale
    grad_second = contract_first(hidden, grad_all) * scale
    row_ids = touched_ids[0]
    old_rows = table[0][row_ids]
    old_acc = accum[0][row_ids]
    new_acc = old_acc + jnp.mean(row_grad * row_grad, axis=-1)
    new_row = old_rows - 0.5 * row_grad / (jnp.sqrt(new_acc)[:, None] + 1e-08)
    return (grad_first[None], grad_second[None], new_row[None], new_acc[None])


def solution(mesh):
    in_specs = (
        P("tower", "shard", None),
        P(("tower", "shard"), None, None),
        P("tower", "shard", None),
        P("tower", "shard", None),
        P("tower", "shard", None),
        P("tower", "shard"),
        P("tower", "shard"),
        P("tower", None, None, None),
        P("tower", None, None, None),
    )
    out_specs = (
        P("tower", "shard", None),
        P("tower", "shard", None),
        P("tower", "shard", None),
        P("tower", "shard"),
    )
    return jax.shard_map(shards, mesh=mesh, in_specs=in_specs, out_specs=out_specs, check_vma=False)
```

```python
import jax
import jax.numpy as jnp
from jax import lax
from jax.experimental import pallas as pl
from jax.experimental.pallas import tpu as pltpu
from jax.sharding import PartitionSpec as P

EMB = 128
FEAT = 100
TOUCHED = 256
MESH = pl.DeviceIdType.MESH
VMEM = pltpu.VMEM
DMA = pltpu.SemaphoreType.DMA
NZ = 8
BF = jnp.bfloat16
F32 = jnp.float32


def contract_first(left, right):
    return lax.dot_general(left, right, (((0,), (0,)), ((), ())), preferred_element_type=F32)


def contract_last(left, right):
    return lax.dot_general(left, right, (((1,), (1,)), ((), ())), preferred_element_type=F32)


def place():
    s = lax.axis_index("shard")
    return s, s // 16, (s // 2) % NZ, s % 2


def shard_of(y, z, c):
    return y * 16 + z * 2 + c


def shard_id(s):
    return {"shard": s}


def remote(src, dst, send, recv, where):
    return pltpu.make_async_remote_copy(
        src_ref=src, dst_ref=dst, send_sem=send, recv_sem=recv, device_id=where, device_id_type=MESH
    )


def tower_kernel(
    pooled, w, w2, dout, bags, slots,
    big, counts, gall, bp_out, hid_out, out,
    bag_v, slot_v, dgot, stage, w_v, xblk, wq,
    bpall, acc, send1, recv1, flat, cv, mate_out, mate_in, own_rows, send2, recv2, yout, yin,
    in_sem, dsend, drecv, loc_sem, out_sem, xsem,
    first_send, first_recv, ring_send, ring_recv, mate_send, mate_recv, wsend, wrecv,
    bsend, brecv, ssem1, rsem1, csem, msend, mrecv, ssem2, rsem2, ysem,
):
    t = lax.axis_index("tower")
    s, y, z, c = place()
    towers = dout.shape[0]
    samples, cols = pooled.shape
    hid = w.shape[0]
    quarter = wq.shape[1]
    half = cols // 2
    rows = 4 * samples
    mate, other, diag = shard_of(y, z, 1 - c), shard_of(1 - y, z, c), shard_of(1 - y, z, 1 - c)
    ahead, behind = shard_of(y, (z + 1) % NZ, c), shard_of(y, (z + NZ - 1) % NZ, c)
    peers = (ahead, behind)
    me4 = y * 2 + c
    me_hid = pl.multiple_of(me4 * hid, hid)

    load_w = pltpu.make_async_copy(w, w_v, in_sem.at[2])
    load_bags = pltpu.make_async_copy(bags, bag_v, in_sem.at[0])
    load_slots = pltpu.make_async_copy(slots, slot_v, in_sem.at[1])
    load_bags.start()
    load_slots.start()
    load_w.start()

    barrier = pltpu.get_barrier_semaphore()
    for peer in (mate, other, diag, ahead, behind):
        pl.semaphore_signal(barrier, inc=1, device_id=shard_id(peer), device_id_type=MESH)
    for step in range(1, towers):
        pl.semaphore_signal(barrier, inc=1, device_id={"tower": (t + step) % towers}, device_id_type=MESH)
    pl.semaphore_wait(barrier, 5 + towers - 1)

    sent = []

    def block(zz, yy):
        return zz * 4 + yy * 2 + c

    def go(copy):
        copy.start()
        sent.append(copy)
        return copy

    mine = block(z, y)
    pending = {}

    def note(label, copy):
        pending.setdefault(label, []).append(copy)

    tile_rows = dout.shape[1]
    land = dgot.at[pl.ds(pl.multiple_of(t * tile_rows, tile_rows), tile_rows), :]
    dcopies = []
    for step in range(1, towers):
        u = (t + step) % towers
        dcopies.append(go(remote(dout.at[u], land, dsend.at[step], drecv.at[step], {"tower": u})))
    own_d = pltpu.make_async_copy(dout.at[t], land, loc_sem.at[0])
    own_d.start()

    firsts = []
    for i, peer in enumerate((ahead, behind, other)):
        firsts.append(go(remote(pooled, big.at[mine], first_send.at[0, i], first_recv.at[0, i], shard_id(peer))))
    note(0, go(remote(pooled, big.at[mine], mate_send.at[0, 0], mate_recv.at[0, 0], shard_id(mate))))
    own_p = pltpu.make_async_copy(pooled, big.at[mine], loc_sem.at[1])
    own_p.start()

    own_d.wait()
    for copy in dcopies:
        copy.wait_recv()
    per = gall.shape[2] // EMB
    for k in range(per):
        gall[mine, :, k * EMB:(k + 1) * EMB] = dgot[pl.ds(k, samples, stride=per), :].astype(BF)
    gmine = gall.at[mine]
    for i, peer in enumerate((ahead, behind, other)):
        firsts.append(go(remote(gmine, gmine, first_send.at[1, i], first_recv.at[1, i], shard_id(peer))))
    note(0, go(remote(gmine, gmine, mate_send.at[1, 0], mate_recv.at[1, 0], shard_id(mate))))

    def view(kind, at):
        if kind == 0:
            return big.at[at]
        if kind == 1:
            return gall.at[at]
        return big.at[at, :, pl.ds((kind - 2) * half, half)]

    mate_slot = [1, 1]

    def to_mate(kind, at, label):
        row = 1 if kind == 1 else 0
        slot = mate_slot[row]
        mate_slot[row] += 1
        note(label, go(remote(
            view(kind, at), view(kind, at), mate_send.at[row, slot], mate_recv.at[row, slot], shard_id(mate))))

    ring_copies = {}

    def to_ring(kind, at, hop, direction, chain):
        row = 1 if kind == 1 else 0
        index = (hop - 1) * 4 + direction * 2 + chain
        ring_copies[(row, hop, direction, chain)] = go(remote(
            view(kind, at), view(kind, at), ring_send.at[row, index], ring_recv.at[row, index],
            shard_id(peers[direction])))

    yblock = block(z, 1 - y)
    firsts[2].wait_recv()
    for direction in range(2):
        to_ring(0, yblock, 1, direction, 1)
    to_mate(0, yblock, 0)
    firsts[5].wait_recv()
    for direction in range(2):
        to_ring(1, yblock, 1, direction, 1)
    to_mate(1, yblock, 0)

    wcopies = []
    for i, (yy, cc, peer) in enumerate(((y, 1 - c, mate), (1 - y, c, other), (1 - y, 1 - c, diag))):
        part = pl.multiple_of((yy * 2 + cc) * quarter, EMB)
        wcopies.append(go(remote(
            w.at[:, pl.ds(part, quarter)], wq.at[pl.ds(me_hid, hid), :], wsend.at[i], wrecv.at[i], shard_id(peer))))
    own_w = pltpu.make_async_copy(
        w.at[:, pl.ds(pl.multiple_of(me4 * quarter, EMB), quarter)], wq.at[pl.ds(me_hid, hid), :], loc_sem.at[3])
    own_w.start()

    load_bags.wait()
    load_slots.wait()
    load_w.wait()
    look = bags.shape[2]
    pad = stage.shape[2] // 4
    local_feat = quarter // EMB
    low = me4 * local_feat

    def owner_counts(owner, slot_at):
        @pl.when(owner >= 2)
        def _():
            pltpu.make_async_copy(stage.at[slot_at], counts.at[owner], out_sem.at[slot_at]).wait()

        for i in range(4):
            source = shard_of(i // 2, z, i % 2)
            bag = bag_v[owner, pl.ds(source, 1), :]
            slot = slot_v[owner, pl.ds(source, 1), :]
            sample = (bag * 5243) >> 19
            feat = bag - sample * FEAT - low
            ok = (feat >= 0) & (feat < local_feat)
            bag_local = jnp.where(ok, feat * samples + sample, -1)
            left = (lax.broadcasted_iota(jnp.int32, (TOUCHED, look), 0) == slot).astype(F32).astype(BF)
            right = (lax.broadcasted_iota(jnp.int32, (pad, look), 0) == bag_local).astype(F32).astype(BF)
            stage[slot_at, :, i * pad:(i + 1) * pad] = contract_last(left, right).astype(BF)
        pltpu.make_async_copy(stage.at[slot_at], counts.at[owner], out_sem.at[slot_at]).start()

    owners = bags.shape[0]
    done = [0]

    def count_some(pairs):
        start = done[0]
        done[0] += pairs

        def body(p, carry):
            owner_counts(p * 2, 0)
            owner_counts(p * 2 + 1, 1)
            return carry

        lax.fori_loop(start, start + pairs, body, 0)

    def load_slab(label, zz, at):
        for copy in pending.pop(label):
            copy.wait_recv()
        load = pltpu.make_async_copy(big.at[pl.ds(zz * 4, 4)], xblk.at[at], xsem.at[at])
        load.start()
        return load

    bp_copies = {}
    step_k = cols // 10 if cols % (10 * EMB) == 0 else EMB

    def tower_step(loads, zs, names):
        m = len(zs)
        for load in loads:
            load.wait()

        def body(i, total):
            at = pl.ds(pl.multiple_of(i * step_k, EMB), step_k)
            left = xblk[0:m, :, :, at].reshape(m * rows, step_k)
            return total + contract_last(left, w_v[:, at])

        pre = lax.fori_loop(0, cols // step_k, body, jnp.zeros((m * rows, hid), F32))
        sig = jax.nn.sigmoid(pre)
        hidden = (pre * sig).astype(BF)
        for i, zz in enumerate(zs):
            part = slice(i * rows, (i + 1) * rows)
            at = pl.ds(pl.multiple_of(zz * rows, rows), rows)
            grads = gall[pl.ds(zz * 4, 4)].reshape(rows, gall.shape[2])
            back_hidden = contract_last(grads, w2[...])
            sg, p = sig[part], pre[part]
            back_pre = (back_hidden * sg * (1.0 + p * (1.0 - sg))).astype(BF)
            hid_out[at, :] = hidden[part]
            bp_out[at, :] = back_pre
            bpall[at, pl.ds(me_hid, hid)] = back_pre
            where = bpall.at[at, pl.ds(me_hid, hid)]
            bp_copies[names[i]] = [
                go(remote(where, where, bsend.at[names[i], j], brecv.at[names[i], j], shard_id(peer)))
                for j, peer in enumerate((other, diag, mate))
            ]

    steps = (4, 3, 5, 2, 6, 1, 7, 0)
    slabs = [(z + step) % NZ for step in steps]
    tile = quarter // 5 if quarter % (5 * EMB) == 0 else EMB
    cut = (quarter // EMB + 1) // 2 * EMB
    spans = ((0, cut), (cut, quarter))
    slab_w = list(wcopies)

    def product(n):
        while slab_w:
            slab_w.pop().wait_recv()
        for copy in bp_copies.pop(steps[n]):
            copy.wait_recv()
        left = bpall[pl.ds(pl.multiple_of(slabs[n] * rows, rows), rows), :]

        def body(i, carry):
            at = pl.ds(pl.multiple_of(i * tile, EMB), tile)
            acc[n % 4, :, at] = jnp.dot(left, wq[:, at], preferred_element_type=F32)
            return carry

        lax.fori_loop(0, quarter // tile, body, 0)

    count_some(3)
    own_p.wait()
    loads = [load_slab(0, z, 0)]
    zs, names = [z], [0]
    for hop in range(1, 4):
        for chain in range(2):
            if chain == 1:
                tower_step(loads, zs, names)
            count_some(2)
            yy = y if chain == 0 else 1 - y
            for direction in range(2):
                zz = (z + hop) % NZ if direction else (z + NZ - hop) % NZ
                at = block(zz, yy)
                label = (hop, direction)
                if hop == 1 and chain == 0:
                    firsts[direction].wait_recv()
                else:
                    ring_copies[(0, hop, direction, chain)].wait_recv()
                to_ring(0 if hop < 3 else 2 + direction, at, hop + 1, direction, chain)
                to_mate(0, at, label)
                if hop == 1 and chain == 0:
                    firsts[3 + direction].wait_recv()
                else:
                    ring_copies[(1, hop, direction, chain)].wait_recv()
                if hop < 3 or direction == 0:
                    to_ring(1, at, hop + 1, direction, chain)
                to_mate(1, at, label)
        if hop == 3:
            count_some(1)
        zs = [(z + NZ - hop) % NZ, (z + hop) % NZ]
        names = [NZ - hop, hop]
        loads = [load_slab((hop, direction), zs[direction], direction) for direction in range(2)]
    own_w.wait()
    tower_step(loads, zs, names)
    for slot_at in range(2):
        pltpu.make_async_copy(stage.at[slot_at], counts.at[owners - 2 + slot_at], out_sem.at[slot_at]).wait()

    depth = cv.shape[0]
    grid = counts.reshape(2, NZ, 2, TOUCHED, 4 * pad)

    def load_counts(n):
        return pltpu.make_async_copy(grid.at[:, slabs[n]], cv.at[n % depth], csem.at[n % depth])

    for n in range(depth):
        load_counts(n).start()
    flat[...] = jnp.zeros_like(flat)
    product(1)
    product(2)
    zz = (z + 4) % NZ
    for chain in range(2):
        yy = y if chain == 0 else 1 - y
        at = block(zz, yy)
        for direction in range(2):
            ring_copies[(0, 4, direction, chain)].wait_recv()
            to_mate(2 + direction, at, 4)
        ring_copies[(1, 4, 0, chain)].wait_recv()
        to_mate(1, at, 4)

    def ring(view, calc, own, send, recv, ssem, rsem, early):
        copies = {}

        def push(direction, h, part, value):
            place_at = view(send, direction, h, part)
            place_at[...] = value.astype(send.dtype)
            index = h * 2 + part
            copies[(direction, h, part)] = go(remote(
                place_at, view(recv, direction, h, part),
                ssem.at[direction, index], rsem.at[direction, index], shard_id(peers[direction])))

        def got(direction, h, part):
            copies[(direction, h, part)].wait_recv()
            return view(recv, direction, h, part)[...].astype(F32)

        if early:
            push(0, 1, 1, own(1, 1))
            push(1, 1, 0, own(2, 0))
        calc(0)
        push(0, 0, 0, own(0, 0))
        push(1, 0, 1, own(0, 1))
        if not early:
            calc(1)
            calc(2)
            push(0, 1, 1, own(1, 1))
            push(1, 1, 0, own(2, 0))
        calc(3)
        calc(4)
        push(0, 1, 0, own(1, 0) + got(0, 0, 0))
        push(1, 1, 1, own(2, 1) + got(1, 0, 1))
        calc(5)
        calc(6)
        for h in (2, 3):
            n = 2 * h - 1
            push(0, h, 1, own(n, 1) + got(0, h - 1, 1))
            push(1, h, 0, own(n + 1, 0) + got(1, h - 1, 0))
            push(0, h, 0, own(n, 0) + got(0, h - 1, 0))
            push(1, h, 1, own(n + 1, 1) + got(1, h - 1, 1))
            if h == 2:
                calc(7)

        def final(part):
            return own(7, part) + got(0, 3, part) + got(1, 3, part)

        return final

    def view1(buf, direction, h, part):
        return buf.at[direction, h, :, spans[part][0]:spans[part][1]]

    def own1(n, part):
        return acc[n % 4, :, spans[part][0]:spans[part][1]]

    def calc1(n):
        if n == 0:
            tower_step([load_slab(4, zz, 0)], [zz], [4])
        product(n)

    final = ring(view1, calc1, own1, send1, recv1, ssem1, rsem1, True)
    for part in (1, 0):
        total = final(part).astype(BF)
        for f in range(spans[part][0] // EMB, spans[part][1] // EMB):
            at = f * EMB - spans[part][0]
            for i in range(4):
                flat[i, f * samples:(f + 1) * samples, :] = total[i * samples:(i + 1) * samples, at:at + EMB]

    local_bags = flat.shape[0] * flat.shape[1]
    mates = {}

    def row_sums(n):
        load_counts(n).wait()
        for yy in range(2):
            mate_out[n, yy] = jnp.dot(
                cv[n % depth, yy, 1 - c], flat[...].reshape(local_bags, EMB), preferred_element_type=F32)
        mates[n] = go(remote(mate_out.at[n], mate_in.at[n], msend.at[n], mrecv.at[n], shard_id(mate)))
        for yy in range(2):
            own_rows[n, yy] = jnp.dot(
                cv[n % depth, yy, c], flat[...].reshape(local_bags, EMB), preferred_element_type=F32)
        if n + depth < NZ:
            load_counts(n + depth).start()

    def calc2(n):
        if n == 0:
            row_sums(0)
            row_sums(1)
        elif n > 1:
            row_sums(n)

    def view2(buf, direction, h, part):
        return buf.at[direction, h, part]

    def own2(n, part):
        if n in mates:
            mates.pop(n).wait_recv()
        return own_rows[n, part] + mate_in[n, part]

    final = ring(view2, calc2, own2, send2, recv2, ssem2, rsem2, False)
    sums = [final(0), final(1)]
    yout[...] = jnp.where(y == 0, sums[1], sums[0])
    last = go(remote(yout, yin, ysem.at[0], ysem.at[1], shard_id(other)))
    kept = jnp.where(y == 0, sums[0], sums[1])
    last.wait_recv()
    out[...] = kept + yin[...]
    for copy in sent:
        copy.wait_send()


def tower_all(pooled, w, w2, dout, bags, slots):
    samples, cols = pooled.shape
    hid = w.shape[0]
    n_shard = bags.shape[0]
    batch = n_shard * samples
    out = w2.shape[1]
    quarter = cols // 4
    rows = 4 * samples
    pad = -(-(quarter // EMB * samples) // 512) * 512
    any_spec = pl.BlockSpec(memory_space=pl.ANY)
    vm = pl.BlockSpec(memory_space=VMEM)
    depth = 3
    return pl.pallas_call(
        tower_kernel,
        out_shape=(
            jax.ShapeDtypeStruct((n_shard, samples, cols), BF),
            jax.ShapeDtypeStruct((n_shard, TOUCHED, 4 * pad), BF),
            jax.ShapeDtypeStruct((n_shard, samples, out), BF),
            jax.ShapeDtypeStruct((batch, hid), BF),
            jax.ShapeDtypeStruct((batch, hid), BF),
            jax.ShapeDtypeStruct((TOUCHED, EMB), F32),
        ),
        in_specs=[any_spec, any_spec, vm, any_spec, any_spec, any_spec],
        out_specs=(any_spec, any_spec, vm, vm, vm, vm),
        scratch_shapes=[
            VMEM(bags.shape, jnp.int32),
            VMEM(slots.shape, jnp.int32),
            VMEM((dout.shape[0] * dout.shape[1], EMB), F32),
            VMEM((2, TOUCHED, 4 * pad), BF),
            VMEM((hid, cols), BF),
            VMEM((2, 4, samples, cols), BF),
            VMEM((4 * hid, quarter), BF),
            VMEM((batch, 4 * hid), BF),
            VMEM((4, rows, quarter), F32),
            VMEM((2, 4, rows, quarter), BF),
            VMEM((2, 4, rows, quarter), BF),
            VMEM((4, pad, EMB), BF),
            VMEM((depth, 2, 2, TOUCHED, 4 * pad), BF),
            VMEM((NZ, 2, TOUCHED, EMB), F32),
            VMEM((NZ, 2, TOUCHED, EMB), F32),
            VMEM((NZ, 2, TOUCHED, EMB), F32),
            VMEM((2, 4, 2, TOUCHED, EMB), BF),
            VMEM((2, 4, 2, TOUCHED, EMB), BF),
            VMEM((TOUCHED, EMB), F32),
            VMEM((TOUCHED, EMB), F32),
            DMA((3,)), DMA((8,)), DMA((8,)), DMA((4,)), DMA((2,)), DMA((2,)),
            DMA((2, 3)), DMA((2, 3)), DMA((2, 16)), DMA((2, 16)), DMA((2, 18)), DMA((2, 18)), DMA((3,)), DMA((3,)),
            DMA((8, 3)), DMA((8, 3)), DMA((2, 8)), DMA((2, 8)), DMA((depth,)), DMA((8,)), DMA((8,)),
            DMA((2, 8)), DMA((2, 8)), DMA((2,)),
        ],
        compiler_params=pltpu.CompilerParams(
            collective_id=0, has_side_effects=True, vmem_limit_bytes=60 * 1024 * 1024
        ),
        name="tower",
    )(pooled, w, w2, dout, bags, slots)


def shards(pooled, dout, w_first, w_second, table, accum, touched_ids, lookup_bag, lookup_slot):
    towers = dout.shape[1]
    samples = pooled.shape[1]
    dtiles = jnp.transpose(dout, (1, 0, 2)).astype(F32).reshape(towers, -1, EMB)
    big, _, gall, back_pre, hidden, row_grad = tower_all(
        pooled[0], w_first[0], w_second[0], dtiles, lookup_bag[0], lookup_slot[0])
    n_shard = big.shape[0]
    inputs_all = big.reshape(n_shard * samples, -1)
    grad_all = gall.reshape(n_shard * samples, -1)
    scale = float(samples * n_shard) ** (-0.5)
    grad_first = contract_first(back_pre, inputs_all) * scale
    grad_second = contract_first(hidden, grad_all) * scale
    row_ids = touched_ids[0]
    old_rows = table[0][row_ids]
    old_acc = accum[0][row_ids]
    new_acc = old_acc + jnp.mean(row_grad * row_grad, axis=-1)
    new_row = old_rows - 0.5 * row_grad / (jnp.sqrt(new_acc)[:, None] + 1e-08)
    return (grad_first[None], grad_second[None], new_row[None], new_acc[None])


def solution(mesh):
    in_specs = (
        P("tower", "shard", None),
        P(("tower", "shard"), None, None),
        P("tower", "shard", None),
        P("tower", "shard", None),
        P("tower", "shard", None),
        P("tower", "shard"),
        P("tower", "shard"),
        P("tower", None, None, None),
        P("tower", None, None, None),
    )
    out_specs = (
        P("tower", "shard", None),
        P("tower", "shard", None),
        P("tower", "shard", None),
        P("tower", "shard"),
    )
    return jax.shard_map(shards, mesh=mesh, in_specs=in_specs, out_specs=out_specs, check_vma=False)
```
